512 devices in a mesh: tile: 128 (over y, z_hi, x), lev: 4 (over z_lo, core).
Axes of the slice: x: 4, y: 8, z: 8 (z_hi: 4, z_lo: 2; z = z_hi * 2 + z_lo), core: 2. Of those that a mesh axis runs over, the one named last changes fastest.
Arguments:
- tracers: float32 [384, 4, 64, 1024], P('tile', 'lev'), may hold values from -6 to 6
- courant_x: float32 [384, 4, 64, 65], P('tile', 'lev'), may hold values from -0.2 to 0.2
- courant_y: float32 [384, 4, 65, 64], P('tile', 'lev'), may hold values from -0.2 to 0.2
- cell_area: float32 [384, 64, 64], P('tile'), may hold values from 0.5 to 1.5
- neighbor: int32 [384, 4], replicated, may hold values from 0 to 383, as said below
- rotation: int32 [384, 4], replicated, may hold values from 0 to 7, as said below
- weights: float32 [384, 4, 128], P('tile', 'lev'), may hold values from 0.1 to 1
- sounding_column: int32 [384, 128], P('tile'), may hold values from 0 to 4095
- sounding_count: int32 [384], P('tile'), may hold values from 1 to 128
Outputs:
- transported: float32 [384, 4, 64, 1024], P('tile', 'lev')
- column_mean: float32 [384, 16, 128], P('tile')
The draws below stay inside these ranges and needn't reach their ends.
Inputs may be any that keep to these rules, and one draw needn't show every extreme that they name: `neighbor`: neighbor and rotation describe the edges of a cubed sphere of 6 faces of equal square grids of tiles; tile i lies on index i // 3 of tile. The edge strips that the tiles of one index of tile take from the tiles of another index number at most 3. The rotation codes belong to the same cubed sphere as neighbor.
All inputs are finite; a program needn't handle non-finite values.
Results may differ from the reference program's by a relative error of at most 0.00002.
Values sent between devices are 32-bit elements; how exact they have to be, the bound alone decides.
A program may use at most 64 MiB of HBM per device.

```python
import math
import jax
import jax.numpy as jnp
import numpy as np

TR = 16
S = 64
NS = 128
STEPS = 2
TILES_DEV = 3
TILES = 384
LEVELS = 4


def cube_table(side):
    normals = np.array([[1, 0, 0], [0, 1, 0], [-1, 0, 0], [0, -1, 0], [0, 0, 1], [0, 0, -1]], np.float32)
    axes_a = np.array([[0, 1, 0], [-1, 0, 0], [0, -1, 0], [1, 0, 0], [0, 1, 0], [0, 1, 0]], np.float32)
    axes_b = np.array([[0, 0, 1], [0, 0, 1], [0, 0, 1], [0, 0, 1], [-1, 0, 0], [1, 0, 0]], np.float32)
    count_all = 6 * side * side
    partner = np.zeros((count_all, 4), np.int32)
    codes = np.zeros((count_all, 4), np.int32)
    for face in range(6):
        for row in range(side):
            for col in range(side):
                base = face * side * side + row * side + col
                s_mid = (col + 0.5) / side * 2.0 - 1.0
                t_mid = (row + 0.5) / side * 2.0 - 1.0
                for edge in range(4):
                    if edge == 0 and col > 0:
                        partner[base, edge] = base - 1
                        codes[base, edge] = 1
                        continue
                    if edge == 1 and col < side - 1:
                        partner[base, edge] = base + 1
                        codes[base, edge] = 0
                        continue
                    if edge == 2 and row > 0:
                        partner[base, edge] = base - side
                        codes[base, edge] = 3
                        continue
                    if edge == 3 and row < side - 1:
                        partner[base, edge] = base + side
                        codes[base, edge] = 2
                        continue
                    if edge == 0:
                        s_at, t_at, outward, along = (-1.0, t_mid, -axes_a[face], axes_b[face])
                    elif edge == 1:
                        s_at, t_at, outward, along = (1.0, t_mid, axes_a[face], axes_b[face])
                    elif edge == 2:
                        s_at, t_at, outward, along = (s_mid, -1.0, -axes_b[face], axes_a[face])
                    else:
                        s_at, t_at, outward, along = (s_mid, 1.0, axes_b[face], axes_a[face])
                    point = normals[face] + s_at * axes_a[face] + t_at * axes_b[face]
                    target = int(np.argmax(normals @ outward))
                    s_new = float(point @ axes_a[target])
                    t_new = float(point @ axes_b[target])
                    if abs(s_new + 1.0) < 1e-06:
                        other_edge, new_col = (0, 0)
                        new_row = min(side - 1, int(math.floor((t_new + 1.0) / 2.0 * side)))
                        their_along = axes_b[target]
                    elif abs(s_new - 1.0) < 1e-06:
                        other_edge, new_col = (1, side - 1)
                        new_row = min(side - 1, int(math.floor((t_new + 1.0) / 2.0 * side)))
                        their_along = axes_b[target]
                    elif abs(t_new + 1.0) < 1e-06:
                        other_edge, new_row = (2, 0)
                        new_col = min(side - 1, int(math.floor((s_new + 1.0) / 2.0 * side)))
                        their_along = axes_a[target]
                    else:
                        other_edge, new_row = (3, side - 1)
                        new_col = min(side - 1, int(math.floor((s_new + 1.0) / 2.0 * side)))
                        their_along = axes_a[target]
                    reversed_flag = 1 if float(along @ their_along) < 0.0 else 0
                    partner[base, edge] = target * side * side + new_row * side + new_col
                    codes[base, edge] = other_edge + 4 * reversed_flag
    return (partner, codes)


def placed_table(key):
    side = math.isqrt(TILES // 6)
    partner, codes = cube_table(side)
    groups = TILES // TILES_DEV
    order = jax.random.permutation(jax.random.fold_in(key, 7), groups)
    inverse = jnp.argsort(order)
    slots = jnp.arange(TILES)
    base_of_slot = TILES_DEV * order[slots // TILES_DEV] + slots % TILES_DEV
    base_partner = jnp.asarray(partner)[base_of_slot]
    slot_partner = TILES_DEV * inverse[base_partner // TILES_DEV] + base_partner % TILES_DEV
    return (slot_partner.astype(jnp.int32), jnp.asarray(codes)[base_of_slot].astype(jnp.int32))


def draw_neighbor(key, part):
    return placed_table(key)[0]


def draw_rotation(key, part):
    return placed_table(key)[1]


def set_ends(drawn, stream_key, low, largest):
    extent = drawn.shape
    index_at = [jax.random.randint(jax.random.fold_in(stream_key, axis), (), 0, extent[axis]) for axis in range(len(extent))]
    drawn = drawn.at[tuple(index_at)].set(low)
    longest = extent.index(max(extent))
    index_at[longest] = (index_at[longest] + 1) % extent[longest]
    return drawn.at[tuple(index_at)].set(largest)


def level_of(key, dims, shards, low, top_value):
    loudness, own = 1.0, jax.random.fold_in(key, 6)
    for position, shards_of in shards:
        draws = jnp.exp(jax.random.uniform(jax.random.fold_in(own, position), (shards_of,), jnp.float32, low / len(shards), top_value / len(shards)))
        loudness = loudness * jnp.repeat(draws, dims[position] // shards_of).reshape([-1 if axis == position else 1 for axis in range(len(dims))])
    return loudness


def noise(rng, extent, scale, most, pieces=(), kind=jnp.bfloat16):
    values = jax.random.normal(rng, extent, jnp.float32) * scale
    if len(pieces) > 0:
        values = level_of(rng, extent, pieces, -0.22, 0.18) * values
    return jnp.clip(values, min=-most, max=most).astype(kind)


def setup_inputs(seed: int = 0) -> dict:
    key_of = jax.random.split(jax.random.key(seed), 10)
    return {
        "tracers": noise(key_of[0], (TILES, LEVELS, S, S * TR), 1.0, 6.0, ((0, 128), (1, 4)), jnp.float32),
        "courant_x": jnp.clip(jax.random.uniform(key_of[1], (TILES, LEVELS, S, S + 1), jnp.float32, -0.2, 0.2) * level_of(key_of[1], (TILES, LEVELS, S, S + 1), ((0, 128), (1, 4)), -0.4, 0.0), -0.2, 0.2),
        "courant_y": jnp.clip(jax.random.uniform(key_of[2], (TILES, LEVELS, S + 1, S), jnp.float32, -0.2, 0.2) * level_of(key_of[2], (TILES, LEVELS, S + 1, S), ((0, 128), (1, 4)), -0.4, 0.0), -0.2, 0.2),
        "cell_area": jnp.clip(1.0 + 0.1 * jax.random.normal(key_of[3], (TILES, S, S), jnp.float32), 0.5, 1.5),
        "neighbor": draw_neighbor(jax.random.fold_in(key_of[9], 71), 0),
        "rotation": draw_rotation(jax.random.fold_in(key_of[9], 71), 0),
        "weights": jnp.clip(jnp.exp(math.log(1.0) - 2.3025851 * jax.random.uniform(key_of[6], (TILES, LEVELS, NS), jnp.float32) ** level_of(key_of[6], (TILES, LEVELS, NS), ((0, 128), (1, 4)), -0.2, 0.2)), 0.1, 1.0),
        "sounding_column": set_ends(jax.random.randint(key_of[7], (TILES, NS), 0, S * S), jax.random.fold_in(key_of[7], 1), 0, (S * S) - 1).astype(jnp.int32),
        "sounding_count": set_ends(jax.random.randint(key_of[8], (TILES,), 1, NS + 1), jax.random.fold_in(key_of[8], 1), 1, NS).astype(jnp.int32),
    }


def edge_strips(field, members):
    tiles, levels, side, width = field.shape
    west = field[..., :, 0:members]
    east = field[..., :, width - members:]
    south = field[..., 0, :].reshape(tiles, levels, side, members)
    north = field[..., side - 1, :].reshape(tiles, levels, side, members)
    return jnp.stack([west, east, south, north], axis=1)


def surround(field, halos, members):
    tiles, levels, side, width = field.shape
    padded = jnp.pad(field, ((0, 0), (0, 0), (1, 1), (members, members)))
    padded = padded.at[:, :, 1:side + 1, 0:members].set(halos[:, 0])
    padded = padded.at[:, :, 1:side + 1, width + members:].set(halos[:, 1])
    padded = padded.at[:, :, 0, members:width + members].set(halos[:, 2].reshape(tiles, levels, width))
    padded = padded.at[:, :, side + 1, members:width + members].set(halos[:, 3].reshape(tiles, levels, width))
    return padded


def advance(padded, field, courant_x, courant_y, cell_area, members):
    flow_x = jnp.repeat(courant_x, members, axis=3)
    flow_y = jnp.repeat(courant_y, members, axis=3)
    area = jnp.repeat(cell_area, members, axis=2)[:, None]
    flux_x = jnp.maximum(flow_x, 0.0) * padded[:, :, 1:-1, :-members] + jnp.minimum(flow_x, 0.0) * padded[:, :, 1:-1, members:]
    flux_y = jnp.maximum(flow_y, 0.0) * padded[:, :, :-1, members:-members] + jnp.minimum(flow_y, 0.0) * padded[:, :, 1:, members:-members]
    change = (flux_x[..., members:] - flux_x[..., :-members]) + (flux_y[:, :, 1:, :] - flux_y[:, :, :-1, :])
    return field - change / area


def reference(tracers, courant_x, courant_y, cell_area, neighbor, rotation, weights, sounding_column, sounding_count):
    members = TR
    field = tracers
    for step in range(STEPS):
        strips = edge_strips(field, members)
        picked = strips[neighbor, rotation % 4]
        flipped = (rotation // 4 == 1)[:, :, None, None, None]
        halos = jnp.where(flipped, picked[..., ::-1, :], picked)
        field = advance(surround(field, halos, members), field, courant_x, courant_y, cell_area, members)
    tiles, levels, side, width = field.shape
    slots = sounding_column.shape[1]
    flat = field.reshape(tiles, levels, side * side, members)
    index_full = jnp.broadcast_to(sounding_column[:, None, :, None], (tiles, levels, slots, members))
    sampled = jnp.take_along_axis(flat, index_full, axis=2)
    weighted = jnp.sum(weights[:, :, :, None] * sampled, axis=1)
    weighted = jnp.transpose(weighted, (0, 2, 1))
    totals = jnp.sum(weights, axis=1)
    live = jnp.arange(slots)[None, :] < sounding_count[:, None]
    column_mean = jnp.where(live[:, None, :], weighted / totals[:, None, :], 0.0)
    return field, column_mean
```

```python
import functools

import jax
import jax.numpy as jnp
from jax import lax
from jax.experimental import pallas as pl
from jax.experimental.pallas import tpu as pltpu
from jax.sharding import PartitionSpec as P

MESH = pl.DeviceIdType.MESH
STEPS = 2
TILES_DEV = 3
S = 64
TR = 16
W = S * TR
BLOCKS = W // 128
ROWS = S // 8
NA = 16
NB = 8
SLOTS = 12
CAP_A = 6
CAP_B = 7


def lane_gather(x, index):
    return jnp.take_along_axis(x, index, axis=1, mode="promise_in_bounds")


def iota(shape, axis):
    return lax.broadcasted_iota(jnp.int32, shape, axis)


def plan_kernel(nb_ref, rot_ref, plan_ref, load_ref):
    me = lax.axis_index("tile")
    my_b = me // NA
    code = nb_ref[...] * 8 + rot_ref[...]
    code = jnp.concatenate([code, jnp.zeros((code.shape[0], 124), jnp.int32)], axis=1)
    flat = code.T[0:8]
    sub, lane = iota((8, 128), 0), iota((8, 128), 1)
    edges = []
    for r in range(TILES_DEV):
        at = lane * TILES_DEV + r
        picked = jnp.zeros((8, 128), jnp.int32)
        for block in range(TILES_DEV):
            local = at - 128 * block
            inside = (local >= 0) & (local < 128)
            got = lane_gather(flat[:, 128 * block : 128 * block + 128], jnp.where(inside, local, 0))
            picked = jnp.where(inside, got, picked)
        edges.append(picked[0:4])
    table = jnp.concatenate(edges + [jnp.zeros((4, 128), jnp.int32)], axis=0)
    row = iota((16, 128), 0)
    place = iota((16, 128), 1)
    real = row < SLOTS
    tile = table >> 3
    device = (tile * 21846) >> 16
    slot = (tile - device * TILES_DEV) * 4 + (table & 3)
    flip = (table >> 2) & 1
    dev_a = jnp.where(real, device & (NA - 1), -1)
    dev_b = jnp.where(real, device >> 4, -1)

    def ranks(x):
        total = jnp.zeros((16, 128), jnp.int32)
        for j in range(SLOTS):
            total += jnp.where((row > j) & (x == x[j : j + 1, :]), 1, 0)
        return total

    rank_a, rank_b = ranks(dev_a), ranks(dev_b)
    theirs = []
    for half in range(2):
        part = slice(8 * half, 8 * half + 8)
        got = jnp.zeros((8, 128), jnp.int32)
        for j in range(SLOTS):
            source = jnp.broadcast_to(rank_a[j : j + 1, :], (8, 128))
            got = jnp.where(slot[part] == j, lane_gather(source, device[part]), got)
        theirs.append(got)
    where_a = dev_a * SLOTS + jnp.concatenate(theirs, axis=0)

    def mine(x):
        index = jnp.full((8, 128), me, jnp.int32)
        return jnp.concatenate([lane_gather(x[0:8], index), lane_gather(x[8:16], index)], axis=0)

    my_dev_a, my_dev_b, my_rank_a, my_rank_b = mine(dev_a), mine(dev_b), mine(rank_a), mine(rank_b)
    pack = jnp.zeros((16, 128), jnp.int32)
    forward = jnp.zeros((16, 128), jnp.int32)
    for j in range(SLOTS):
        one = slice(j, j + 1)
        pack += jnp.where((my_dev_a[one] == place) & (my_rank_a[one] == row), j, 0)
        forward += jnp.where((dev_b[one] == my_b) & (rank_b[one] == row), where_a[one], 0)
    plan_ref[0:16, :] = pack
    plan_ref[16:32, :] = forward
    plan_ref[32:48, :] = jnp.where(real, my_dev_b * SLOTS + my_rank_b, 0)
    plan_ref[48:64, :] = mine(flip)
    over_a = jnp.where(real & (dev_a != (place & (NA - 1))) & (rank_a >= CAP_A), 1.0, 0.0)
    over_b = jnp.where(real & (dev_b != (place >> 4)) & (rank_b >= CAP_B), 1.0, 0.0)
    load_ref[0, 0] = jnp.max(jnp.maximum(over_a, over_b))


def main_kernel(
    cap_a,
    cap_b,
    plan_ref,
    count_ref,
    q_ref,
    cx_ref,
    cy_ref,
    area_ref,
    w_ref,
    column_ref,
    out_ref,
    mean_ref,
    field,
    side_w,
    side_e,
    coef,
    strips,
    send_a,
    send_b,
    got_a0,
    got_a1,
    got_b0,
    got_b1,
    level_sum,
    sem_sa,
    sem_ra,
    sem_sb,
    sem_rb,
    sem_sl,
    sem_rl,
):
    me, lev = lax.axis_index("tile"), lax.axis_index("lev")
    my_a, my_b = lax.rem(me, NA), me // NA
    peers_a = [lax.rem(my_a + k, NA) for k in range(NA)]
    peers_b = [lax.rem(my_b + k, NB) for k in range(NB)]
    peers_l = [lax.rem(lev + k, 4) for k in range(4)]

    got_a, got_b = (got_a0, got_a1), (got_b0, got_b1)

    barrier = pltpu.get_barrier_semaphore()
    everyone = [(my_b * NA + a, lev) for a in peers_a[1:]]
    everyone += [(b * NA + my_a, lev) for b in peers_b[1:]]
    everyone += [(me, other) for other in peers_l[1:]]
    for target in everyone:
        pl.semaphore_signal(barrier, inc=1, device_id=target, device_id_type=MESH)

    sub, lane = iota((8, 128), 0), iota((8, 128), 1)
    group, member = lane // TR, lane % TR
    last = 128 - TR

    for t in range(TILES_DEV):
        field[0, t, 8:72, :] = q_ref[t]

    def cut_strips(step):
        for t in range(TILES_DEV):
            for r in range(ROWS):
                rows = slice(8 + 8 * r, 16 + 8 * r)
                for e, start, shift in ((0, 0, 0), (1, W - 128, last)):
                    block = field[step, t, rows, start : start + 128]
                    spread = lane_gather(block, member + shift)
                    line = jnp.sum(jnp.where(group == sub, spread, 0.0), axis=0, keepdims=True)
                    strips[4 * t + e, r : r + 1, :] = line
                block = slice(128 * r, 128 * r + 128)
                strips[4 * t + 2, r : r + 1, :] = field[step, t, 8:9, block]
                strips[4 * t + 3, r : r + 1, :] = field[step, t, 71:72, block]

    def first_hop(step):
        for a in range(NA):
            for k in range(cap_a):
                send_a[step, a, k] = strips[plan_ref[k, a]]
        for k in range(SLOTS):
            got_a[step][my_a * SLOTS + k] = strips[plan_ref[k, my_a]]
        copies = []
        for k in range(1, NA):
            copies.append(
                pltpu.make_async_remote_copy(
                    src_ref=send_a.at[step, peers_a[k], pl.ds(0, cap_a)],
                    dst_ref=got_a[step].at[pl.ds(my_a * SLOTS, cap_a)],
                    send_sem=sem_sa.at[step, k],
                    recv_sem=sem_ra.at[step, k],
                    device_id=(my_b * NA + peers_a[k], lev),
                    device_id_type=MESH,
                )
            )
            copies[-1].start()
        return copies

    def second_hop(step):
        for b in range(NB):
            for k in range(cap_b):
                send_b[step, b, k] = got_a[step][plan_ref[16 + k, b * NA + my_a]]
        for k in range(SLOTS):
            got_b[step][my_b * SLOTS + k] = got_a[step][plan_ref[16 + k, me]]
        copies = []
        for k in range(1, NB):
            copies.append(
                pltpu.make_async_remote_copy(
                    src_ref=send_b.at[step, peers_b[k], pl.ds(0, cap_b)],
                    dst_ref=got_b[step].at[pl.ds(my_b * SLOTS, cap_b)],
                    send_sem=sem_sb.at[step, k],
                    recv_sem=sem_rb.at[step, k],
                    device_id=(peers_b[k] * NA + my_a, lev),
                    device_id_type=MESH,
                )
            )
            copies[-1].start()
        return copies

    def place_halos(step):
        for t in range(TILES_DEV):
            for e in range(4):
                i = 4 * t + e
                strip = got_b[step][plan_ref[32 + i, 0]]
                turned = lane_gather(strip, last - TR * group + member)
                flipped = jnp.full((1, 128), plan_ref[48 + i, 0], jnp.int32) == 1
                for r in range(ROWS):
                    line = jnp.where(flipped, turned[7 - r : 8 - r], strip[r : r + 1])
                    if e < 2:
                        side = side_w if e == 0 else side_e
                        spread = lane_gather(jnp.broadcast_to(line, (8, 128)), TR * sub + member)
                        side[t, 8 * r : 8 * r + 8, :] = spread
                    else:
                        at = 7 if e == 2 else 72
                        field[step, t, at : at + 1, 128 * r : 128 * r + 128] = line

    def coefficients():
        for t in range(TILES_DEV):
            for r in range(ROWS):
                rows = slice(8 * r, 8 * r + 8)
                over = 1.0 / area_ref[t, rows, :]
                cx = cx_ref[t, rows, :]
                west, east = cx[:, 0:S], cx[:, 1 : S + 1]
                south = cy_ref[t, rows, :]
                north = cy_ref[t, 8 * r + 1 : 8 * r + 9, :]
                out = (jnp.maximum(east, 0.0) - jnp.minimum(west, 0.0)) + (
                    jnp.maximum(north, 0.0) - jnp.minimum(south, 0.0)
                )
                compact = (
                    1.0 - out * over,
                    jnp.maximum(west, 0.0) * over,
                    -jnp.minimum(east, 0.0) * over,
                    jnp.maximum(south, 0.0) * over,
                    -jnp.minimum(north, 0.0) * over,
                )
                for n, value in enumerate(compact):
                    wide = jnp.concatenate([value, value], axis=1)
                    for block in range(BLOCKS):
                        coef[n, t, rows, 128 * block : 128 * block + 128] = lane_gather(
                            wide, 8 * block + group
                        )

    def advance(step, write):
        for t in range(TILES_DEV):
            for r in range(ROWS):
                rows = slice(8 * r, 8 * r + 8)
                top = 8 + 8 * r
                cells = [
                    field[step, t, top : top + 8, 128 * b : 128 * b + 128] for b in range(BLOCKS)
                ]
                up = [pltpu.roll(cell, TR, axis=1) for cell in cells]
                down = [pltpu.roll(cell, 128 - TR, axis=1) for cell in cells]
                for b in range(BLOCKS):
                    block = slice(128 * b, 128 * b + 128)
                    before = up[b - 1] if b > 0 else side_w[t, rows, :]
                    after = down[b + 1] if b < BLOCKS - 1 else side_e[t, rows, :]
                    west = jnp.where(lane < TR, before, up[b])
                    east = jnp.where(lane >= last, after, down[b])
                    south = field[step, t, top - 1 : top + 7, block]
                    north = field[step, t, top + 1 : top + 9, block]
                    value = (
                        cells[b] * coef[0, t, rows, block]
                        + (west * coef[1, t, rows, block] + east * coef[2, t, rows, block])
                        + (south * coef[3, t, rows, block] + north * coef[4, t, rows, block])
                    )
                    write(t, rows, block, value)

    def write_next(t, rows, block, value):
        field[1, t, rows.start + 8 : rows.stop + 8, block] = value

    def write_out(t, rows, block, value):
        out_ref[t, rows, block] = value

    cut_strips(0)
    pl.semaphore_wait(barrier, len(everyone))
    sent = []
    for step in range(STEPS):
        if step > 0:
            cut_strips(step)
        copies = first_hop(step)
        sent += copies
        if step == 0:
            coefficients()
        for copy in copies:
            copy.wait_recv()
        copies = second_hop(step)
        sent += copies
        for copy in copies:
            copy.wait_recv()
        place_halos(step)
        advance(step, write_next if step == 0 else write_out)

    mine = level_sum.at[lev]
    for t in range(TILES_DEV):
        column = column_ref[t : t + 1, :]
        weight = w_ref[t : t + 1, :]
        pick = jnp.where(iota((S, 128), 0) == (column >> 6), 1.0, 0.0)
        at = column & (S - 1)
        total = jnp.zeros((TR, 128), jnp.float32)
        for b in range(BLOCKS):
            turned = out_ref[t, :, 128 * b : 128 * b + 128].T
            rows = jnp.dot(
                turned,
                pick,
                preferred_element_type=jnp.float32,
                precision=lax.Precision.HIGHEST,
            )
            for c in range(8):
                total += jnp.where(at == 8 * b + c, rows[TR * c : TR * c + TR], 0.0)
        mine[t, 0:TR, :] = total * weight
        mine[t, TR : TR + 8, :] = jnp.broadcast_to(weight, (8, 128))
    copies = []
    for k in range(1, 4):
        copies.append(
            pltpu.make_async_remote_copy(
                src_ref=level_sum.at[lev],
                dst_ref=level_sum.at[lev],
                send_sem=sem_sl.at[k],
                recv_sem=sem_rl.at[k],
                device_id=(me, peers_l[k]),
                device_id_type=MESH,
            )
        )
        copies[-1].start()
    sent += copies
    for copy in copies:
        copy.wait_recv()
    for t in range(TILES_DEV):
        total = (level_sum[0, t] + level_sum[1, t]) + (level_sum[2, t] + level_sum[3, t])
        live = iota((TR, 128), 1) < count_ref[t]
        mean_ref[t] = jnp.where(live, total[0:TR] / total[TR : TR + 1], 0.0)
    for copy in sent:
        copy.wait_send()


def run_main(cap_a, cap_b, identifier, plan, count, q, cx, cy, area, w, column):
    vmem, smem = pl.BlockSpec(memory_space=pltpu.VMEM), pl.BlockSpec(memory_space=pltpu.SMEM)
    f32 = jnp.float32
    dma = pltpu.SemaphoreType.DMA
    return pl.pallas_call(
        functools.partial(main_kernel, cap_a, cap_b),
        out_shape=(
            jax.ShapeDtypeStruct((TILES_DEV, S, W), f32),
            jax.ShapeDtypeStruct((TILES_DEV, TR, 128), f32),
        ),
        in_specs=[smem] * 2 + [vmem] * 6,
        out_specs=(vmem, vmem),
        scratch_shapes=[
            pltpu.VMEM((2, TILES_DEV, S + 16, W), f32),
            pltpu.VMEM((TILES_DEV, S, 128), f32),
            pltpu.VMEM((TILES_DEV, S, 128), f32),
            pltpu.VMEM((5, TILES_DEV, S, W), f32),
            pltpu.VMEM((SLOTS, 8, 128), f32),
            pltpu.VMEM((2, NA, SLOTS, 8, 128), f32),
            pltpu.VMEM((2, NB, SLOTS, 8, 128), f32),
            pltpu.VMEM((NA * SLOTS, 8, 128), f32),
            pltpu.VMEM((NA * SLOTS, 8, 128), f32),
            pltpu.VMEM((NB * SLOTS, 8, 128), f32),
            pltpu.VMEM((NB * SLOTS, 8, 128), f32),
            pltpu.VMEM((4, TILES_DEV, TR + 8, 128), f32),
            dma((2, NA)),
            dma((2, NA)),
            dma((2, NB)),
            dma((2, NB)),
            dma((4,)),
            dma((4,)),
        ],
        compiler_params=pltpu.CompilerParams(
            collective_id=identifier, has_side_effects=True, vmem_limit_bytes=40 * 2**20
        ),
        name=f"transport_{cap_a}_{cap_b}",
    )(plan, count, q, cx, cy, area, w, column)


def body(
    tracers,
    courant_x,
    courant_y,
    cell_area,
    neighbor,
    rotation,
    weights,
    sounding_column,
    sounding_count,
):
    vmem, smem = pl.BlockSpec(memory_space=pltpu.VMEM), pl.BlockSpec(memory_space=pltpu.SMEM)
    plan, load = pl.pallas_call(
        plan_kernel,
        out_shape=(
            jax.ShapeDtypeStruct((64, 128), jnp.int32),
            jax.ShapeDtypeStruct((1, 1), jnp.float32),
        ),
        in_specs=[vmem, vmem],
        out_specs=(vmem, smem),
        name="plan",
    )(neighbor, rotation)
    operands = (
        plan,
        sounding_count,
        tracers[:, 0],
        courant_x[:, 0],
        courant_y[:, 0],
        cell_area,
        weights[:, 0],
        sounding_column,
    )
    field, mean = lax.cond(
        load[0, 0] > 0.0,
        functools.partial(run_main, SLOTS, SLOTS, 2),
        functools.partial(run_main, CAP_A, CAP_B, 1),
        *operands,
    )
    return field[:, None], mean


def solution(mesh):
    in_specs = (
        P("tile", "lev", None, None),
        P("tile", "lev", None, None),
        P("tile", "lev", None, None),
        P("tile", None, None),
        P(),
        P(),
        P("tile", "lev", None),
        P("tile", None),
        P("tile"),
    )
    out_specs = (P("tile", "lev", None, None), P("tile", None, None))
    return jax.shard_map(body, mesh=mesh, in_specs=in_specs, out_specs=out_specs, check_vma=False)
```

```python
import functools

import jax
import jax.numpy as jnp
from jax import lax
from jax.experimental import pallas as pl
from jax.experimental.pallas import tpu as pltpu
from jax.sharding import PartitionSpec as P

MESH = pl.DeviceIdType.MESH
STEPS = 2
TILES_DEV = 3
S = 64
TR = 16
W = S * TR
BLOCKS = W // 128
ROWS = S // 8
NA = 16
NB = 8
SLOTS = 12
CAP_A = 3
CAP_B = 4
ROUNDS = 3
INSIDE = (NA + NB) * SLOTS


def lane_gather(x, index):
    return jnp.take_along_axis(x, index, axis=1, mode="promise_in_bounds")


def iota(shape, axis):
    return lax.broadcasted_iota(jnp.int32, shape, axis)


def plan_kernel(nb_ref, rot_ref, plan_ref, load_ref):
    me = lax.axis_index("tile")
    my_a, my_b = lax.rem(me, NA), me // NA
    code = nb_ref[...] * 8 + rot_ref[...]
    flat = jnp.concatenate([code, jnp.zeros(code.shape, jnp.int32)], axis=0)
    sub, lane = iota((8, 128), 0), iota((8, 128), 1)
    edges = []
    for r in range(TILES_DEV):
        at = lane * TILES_DEV + r
        picked = jnp.zeros((8, 128), jnp.int32)
        for block in range(TILES_DEV):
            local = at - 128 * block
            inside = (local >= 0) & (local < 128)
            got = lane_gather(flat[:, 128 * block : 128 * block + 128], jnp.where(inside, local, 0))
            picked = jnp.where(inside, got, picked)
        edges.append(picked[0:4])
    table = jnp.concatenate(edges + [jnp.zeros((4, 128), jnp.int32)], axis=0)
    row = iota((16, 128), 0)
    place = iota((16, 128), 1)
    real = row < SLOTS
    tile = table >> 3
    device = (tile * 21846) >> 16
    slot = (tile - device * TILES_DEV) * 4 + (table & 3)
    flip = (table >> 2) & 1
    dev_a = jnp.where(real, device & (NA - 1), -1)
    dev_b = jnp.where(real, device >> 4, -1)
    use_a = jnp.where(real & (dev_a != (place & (NA - 1))), 1, 0)
    use_b = jnp.where(real & (dev_b != (place >> 4)), 1, 0)
    outside = jnp.maximum(use_a, use_b)

    def partner(x):
        parts = []
        for half in range(2):
            part = slice(8 * half, 8 * half + 8)
            got = jnp.zeros((8, 128), jnp.int32)
            for j in range(SLOTS):
                source = jnp.broadcast_to(x[j : j + 1, :], (8, 128))
                got = jnp.where(slot[part] == j, lane_gather(source, device[part]), got)
            parts.append(got)
        return jnp.concatenate(parts, axis=0)

    def count(key, of):
        every, ahead = jnp.zeros((16, 128), jnp.int32), jnp.zeros((16, 128), jnp.int32)
        for j in range(SLOTS):
            one = slice(j, j + 1)
            same = jnp.where(key == key[one], of[one], 0)
            every += same
            ahead += jnp.where(row > j, same, 0)
        return every, ahead

    own, other = place * SLOTS + row, device * SLOTS + slot
    mix = jnp.minimum(own, other) * 5 + jnp.maximum(own, other) * 3
    by_a = jnp.where(own < other, 1, 0) ^ ((mix >> 2) & 1)
    for turn in range(ROUNDS):
        all_a, ahead_a = count(dev_a, by_a * use_a)
        all_b, ahead_b = count(dev_b, (1 - by_a) * use_b)
        first = by_a == 1
        late = jnp.where(
            first, jnp.where(ahead_a >= CAP_A, use_a, 0), jnp.where(ahead_b >= CAP_B, use_b, 0)
        )
        over_a, more_a = jnp.maximum(all_a - CAP_A, 0), jnp.maximum(all_a + 1 - CAP_A, 0)
        over_b, more_b = jnp.maximum(all_b - CAP_B, 0), jnp.maximum(all_b + 1 - CAP_B, 0)
        gain = jnp.where(
            first, over_a * use_a - more_b * use_b, over_b * use_b - more_a * use_a
        )
        theirs = partner((gain + 64) * 2 + late)
        wanted = late | (theirs & 1)
        better = (gain + (theirs >> 1) - 64) > 0
        now = ((mix >> 1) + turn) & 1
        by_a = jnp.where(better & (now == 0), by_a ^ (wanted & outside), by_a)

    go_a, go_b = by_a * outside, (1 - by_a) * outside
    rank_a, rank_b = count(dev_a, go_a)[1], count(dev_b, go_b)[1]
    theirs = partner(rank_a * 16 + rank_b)
    at_a = dev_a * SLOTS + (theirs >> 4)
    at_b = dev_b * SLOTS + (theirs & 15)

    def mine(x):
        index = jnp.full((8, 128), me, jnp.int32)
        return jnp.concatenate([lane_gather(x[0:8], index), lane_gather(x[8:16], index)], axis=0)

    key_a = jnp.where(go_a == 1, dev_a * 16 + rank_a, -1)
    key_b = jnp.where(go_b == 1, dev_b * 16 + rank_b, -1)
    my_key_a, my_key_b = mine(key_a), mine(key_b)
    pack_a, pack_b, forward_a, forward_b = (jnp.zeros((16, 128), jnp.int32) for _ in range(4))
    for j in range(SLOTS):
        one = slice(j, j + 1)
        pack_a += jnp.where(my_key_a[one] == place * 16 + row, j, 0)
        pack_b += jnp.where(my_key_b[one] == place * 16 + row, j, 0)
        forward_a += jnp.where(key_a[one] == my_a * 16 + row, at_b[one], 0)
        forward_b += jnp.where(key_b[one] == my_b * 16 + row, at_a[one], 0)
    take = jnp.where(
        go_a == 1,
        NB * SLOTS + dev_a * SLOTS + rank_a,
        jnp.where(go_b == 1, dev_b * SLOTS + rank_b, (NA + NB) * SLOTS + slot),
    )
    plan_ref[0:16, :] = pack_a
    plan_ref[16:32, :] = pack_b
    plan_ref[32:48, :] = forward_a
    plan_ref[48:64, :] = forward_b
    plan_ref[64:80, :] = mine(jnp.where(real, take * 2 + flip, 0))
    full_a = jnp.where((go_a * use_a == 1) & (rank_a >= CAP_A), 1.0, 0.0)
    full_b = jnp.where((go_b * use_b == 1) & (rank_b >= CAP_B), 1.0, 0.0)
    load_ref[0, 0] = jnp.max(jnp.maximum(full_a, full_b))


def main_kernel(
    cap_a,
    cap_b,
    plan_ref,
    count_ref,
    q_ref,
    cx_ref,
    cy_ref,
    area_ref,
    w_ref,
    column_ref,
    out_ref,
    mean_ref,
    field,
    side_w,
    side_e,
    coef,
    strips,
    send_a,
    send_b,
    got_a0,
    got_a1,
    got_b0,
    got_b1,
    arrived0,
    arrived1,
    level_sum,
    sem_sa,
    sem_ra,
    sem_sb,
    sem_rb,
    sem_sl,
    sem_rl,
):
    me, lev = lax.axis_index("tile"), lax.axis_index("lev")
    my_a, my_b = lax.rem(me, NA), me // NA
    my_z, my_x = my_a // 4, lax.rem(my_a, 4)
    shifts = sorted(range(1, NA), key=lambda k: -2 * min(k // 4, 4 - k // 4) - min(k % 4, 4 - k % 4))
    peers_a = {k: lax.rem(my_z + k // 4, 4) * 4 + lax.rem(my_x + k % 4, 4) for k in shifts}
    peers_b = {k: lax.rem(my_b + k, NB) for k in sorted(range(1, NB), key=lambda k: -min(k, NB - k))}
    peers_l = [lax.rem(lev + k, 4) for k in range(4)]
    got_a, got_b, arrived = (got_a0, got_a1), (got_b0, got_b1), (arrived0, arrived1)

    barrier = pltpu.get_barrier_semaphore()
    everyone = [(my_b * NA + a, lev) for a in peers_a.values()]
    everyone += [(b * NA + my_a, lev) for b in peers_b.values()]
    everyone += [(me, other) for other in peers_l[1:]]
    for target in everyone:
        pl.semaphore_signal(barrier, inc=1, device_id=target, device_id_type=MESH)

    sub, lane = iota((8, 128), 0), iota((8, 128), 1)
    group, member = lane // TR, lane % TR
    last = 128 - TR

    for t in range(TILES_DEV):
        field[0, t, 8:72, :] = q_ref[t]

    def cut_strips(step):
        for t in range(TILES_DEV):
            for r in range(ROWS):
                rows = slice(8 + 8 * r, 16 + 8 * r)
                for e, start, shift in ((0, 0, 0), (1, W - 128, last)):
                    block = field[step, t, rows, start : start + 128]
                    spread = lane_gather(block, member + shift)
                    line = jnp.sum(jnp.where(group == sub, spread, 0.0), axis=0, keepdims=True)
                    strips[4 * t + e, r : r + 1, :] = line
                block = slice(128 * r, 128 * r + 128)
                strips[4 * t + 2, r : r + 1, :] = field[step, t, 8:9, block]
                strips[4 * t + 3, r : r + 1, :] = field[step, t, 71:72, block]

    def move(ref, index, cap, own, source, at, to, base):
        for other in range(index[1]):
            lane = index[2](other)
            for k in range(cap):
                ref[other, k] = source[plan_ref[index[0] + k, lane]]
        for k in range(SLOTS):
            to[base + own * SLOTS + k] = source[plan_ref[index[0] + k, at]]

    def send_in_plane(hop, step, dst, base):
        copies = []
        for k, peer in peers_a.items():
            copies.append(
                pltpu.make_async_remote_copy(
                    src_ref=send_a.at[hop, step, peer, pl.ds(0, cap_a)],
                    dst_ref=dst.at[pl.ds(base + my_a * SLOTS, cap_a)],
                    send_sem=sem_sa.at[hop, step, k],
                    recv_sem=sem_ra.at[hop, step, k],
                    device_id=(my_b * NA + peer, lev),
                    device_id_type=MESH,
                )
            )
            copies[-1].start()
        return copies

    def send_along_y(hop, step, dst, base):
        copies = []
        for k, peer in peers_b.items():
            copies.append(
                pltpu.make_async_remote_copy(
                    src_ref=send_b.at[hop, step, peer, pl.ds(0, cap_b)],
                    dst_ref=dst.at[pl.ds(base + my_b * SLOTS, cap_b)],
                    send_sem=sem_sb.at[hop, step, k],
                    recv_sem=sem_rb.at[hop, step, k],
                    device_id=(peer * NA + my_a, lev),
                    device_id_type=MESH,
                )
            )
            copies[-1].start()
        return copies

    def exchange(step, meanwhile):
        here = arrived[step]
        move(send_a.at[0, step], (0, NA, lambda a: a), cap_a, my_a, strips, my_a, got_a[step], 0)
        one_a = send_in_plane(0, step, got_a[step], 0)
        move(send_b.at[0, step], (16, NB, lambda b: b), cap_b, my_b, strips, my_b, got_b[step], 0)
        one_b = send_along_y(0, step, got_b[step], 0)
        for k in range(SLOTS):
            here[INSIDE + k] = strips[k]
        meanwhile()
        for copy in one_b:
            copy.wait_recv()
        move(
            send_a.at[1, step],
            (32, NA, lambda a: my_b * NA + a),
            cap_a,
            my_a,
            got_b[step],
            me,
            here,
            NB * SLOTS,
        )
        two_a = send_in_plane(1, step, here, NB * SLOTS)
        for copy in one_a:
            copy.wait_recv()
        move(
            send_b.at[1, step],
            (48, NB, lambda b: b * NA + my_a),
            cap_b,
            my_b,
            got_a[step],
            me,
            here,
            0,
        )
        two_b = send_along_y(1, step, here, 0)
        for copy in two_b + two_a:
            copy.wait_recv()
        return one_a + one_b + two_a + two_b

    def place_halos(step):
        for t in range(TILES_DEV):
            for e in range(4):
                i = 4 * t + e
                taken = plan_ref[64 + i, 0]
                strip = arrived[step][taken >> 1]
                turned = lane_gather(strip, last - TR * group + member)
                flipped = jnp.full((1, 128), taken & 1, jnp.int32) == 1
                for r in range(ROWS):
                    line = jnp.where(flipped, turned[7 - r : 8 - r], strip[r : r + 1])
                    if e < 2:
                        side = side_w if e == 0 else side_e
                        spread = lane_gather(jnp.broadcast_to(line, (8, 128)), TR * sub + member)
                        side[t, 8 * r : 8 * r + 8, :] = spread
                    else:
                        at = 7 if e == 2 else 72
                        field[step, t, at : at + 1, 128 * r : 128 * r + 128] = line

    def coefficients():
        at, to = iota((4 * S, W), 0), iota((4 * S, W), 1)
        repeat = jnp.where(((at & (S - 1)) == (to >> 4)) & (at < 3 * S), 1.0, 0.0)
        repeat = repeat.astype(jnp.bfloat16)
        for t in range(TILES_DEV):
            over = 1.0 / area_ref[t]
            cx, cy = cx_ref[t], cy_ref[t].T
            west, east = cx[:, 0:S], cx[:, 1 : S + 1]
            south, north = cy[0:S], cy[1 : S + 1]
            out = (jnp.maximum(east, 0.0) - jnp.minimum(west, 0.0)) + (
                jnp.maximum(north, 0.0) - jnp.minimum(south, 0.0)
            )
            compact = (
                1.0 - out * over,
                jnp.maximum(west, 0.0) * over,
                -jnp.minimum(east, 0.0) * over,
                jnp.maximum(south, 0.0) * over,
                -jnp.minimum(north, 0.0) * over,
            )
            for n, value in enumerate(compact):
                high = value.astype(jnp.bfloat16).astype(jnp.float32)
                rest = value - high
                middle = rest.astype(jnp.bfloat16).astype(jnp.float32)
                parts = [high, middle, rest - middle, jnp.zeros((S, S), jnp.float32)]
                parts = jnp.concatenate(parts, axis=1).astype(jnp.bfloat16)
                coef[n, t] = jnp.dot(parts, repeat, preferred_element_type=jnp.float32)

    def advance(step, write):
        for t in range(TILES_DEV):
            for r in range(ROWS):
                rows = slice(8 * r, 8 * r + 8)
                top = 8 + 8 * r
                cells = [
                    field[step, t, top : top + 8, 128 * b : 128 * b + 128] for b in range(BLOCKS)
                ]
                up = [pltpu.roll(cell, TR, axis=1) for cell in cells]
                down = [pltpu.roll(cell, 128 - TR, axis=1) for cell in cells]
                for b in range(BLOCKS):
                    block = slice(128 * b, 128 * b + 128)
                    before = up[b - 1] if b > 0 else side_w[t, rows, :]
                    after = down[b + 1] if b < BLOCKS - 1 else side_e[t, rows, :]
                    west = jnp.where(lane < TR, before, up[b])
                    east = jnp.where(lane >= last, after, down[b])
                    south = field[step, t, top - 1 : top + 7, block]
                    north = field[step, t, top + 1 : top + 9, block]
                    value = (
                        cells[b] * coef[0, t, rows, block]
                        + (west * coef[1, t, rows, block] + east * coef[2, t, rows, block])
                        + (south * coef[3, t, rows, block] + north * coef[4, t, rows, block])
                    )
                    write(t, rows, block, value)

    def write_next(t, rows, block, value):
        field[1, t, rows.start + 8 : rows.stop + 8, block] = value

    def write_out(t, rows, block, value):
        out_ref[t, rows, block] = value

    cut_strips(0)
    pl.semaphore_wait(barrier, len(everyone))
    sent = []
    for step in range(STEPS):
        if step > 0:
            cut_strips(step)
        sent += exchange(step, coefficients if step == 0 else lambda: None)
        place_halos(step)
        advance(step, write_next if step == 0 else write_out)

    mine = level_sum.at[lev]
    for t in range(TILES_DEV):
        column = column_ref[t : t + 1, :]
        weight = w_ref[t]
        pick = jnp.where(iota((S, 128), 0) == (column >> 6), 1.0, 0.0)
        at = column & (S - 1)
        total = jnp.zeros((TR, 128), jnp.float32)
        for b in range(BLOCKS):
            turned = out_ref[t, :, 128 * b : 128 * b + 128].T
            rows = jnp.dot(
                turned,
                pick,
                preferred_element_type=jnp.float32,
                precision=lax.Precision.HIGHEST,
            )
            for c in range(8):
                total += jnp.where(at == 8 * b + c, rows[TR * c : TR * c + TR], 0.0)
        mine[t, 0:TR, :] = total * weight
        mine[t, TR : TR + 8, :] = jnp.broadcast_to(weight, (8, 128))
    copies = []
    for k in range(1, 4):
        copies.append(
            pltpu.make_async_remote_copy(
                src_ref=level_sum.at[lev],
                dst_ref=level_sum.at[lev],
                send_sem=sem_sl.at[k],
                recv_sem=sem_rl.at[k],
                device_id=(me, peers_l[k]),
                device_id_type=MESH,
            )
        )
        copies[-1].start()
    sent += copies
    for copy in copies:
        copy.wait_recv()
    for t in range(TILES_DEV):
        total = (level_sum[0, t] + level_sum[1, t]) + (level_sum[2, t] + level_sum[3, t])
        live = iota((TR, 128), 1) < count_ref[t]
        mean_ref[t] = jnp.where(live, total[0:TR] / total[TR : TR + 1], 0.0)
    for copy in sent:
        copy.wait_send()


def run_main(cap_a, cap_b, identifier, plan, count, q, cx, cy, area, w, column):
    vmem, smem = pl.BlockSpec(memory_space=pltpu.VMEM), pl.BlockSpec(memory_space=pltpu.SMEM)
    f32 = jnp.float32
    dma = pltpu.SemaphoreType.DMA
    return pl.pallas_call(
        functools.partial(main_kernel, cap_a, cap_b),
        out_shape=(
            jax.ShapeDtypeStruct((TILES_DEV, S, W), f32),
            jax.ShapeDtypeStruct((TILES_DEV, TR, 128), f32),
        ),
        in_specs=[smem] * 2 + [vmem] * 6,
        out_specs=(vmem, vmem),
        scratch_shapes=[
            pltpu.VMEM((2, TILES_DEV, S + 16, W), f32),
            pltpu.VMEM((TILES_DEV, S, 128), f32),
            pltpu.VMEM((TILES_DEV, S, 128), f32),
            pltpu.VMEM((5, TILES_DEV, S, W), f32),
            pltpu.VMEM((SLOTS, 8, 128), f32),
            pltpu.VMEM((2, 2, NA, SLOTS, 8, 128), f32),
            pltpu.VMEM((2, 2, NB, SLOTS, 8, 128), f32),
            pltpu.VMEM((NA * SLOTS, 8, 128), f32),
            pltpu.VMEM((NA * SLOTS, 8, 128), f32),
            pltpu.VMEM((NB * SLOTS, 8, 128), f32),
            pltpu.VMEM((NB * SLOTS, 8, 128), f32),
            pltpu.VMEM((INSIDE + SLOTS, 8, 128), f32),
            pltpu.VMEM((INSIDE + SLOTS, 8, 128), f32),
            pltpu.VMEM((4, TILES_DEV, TR + 8, 128), f32),
            dma((2, 2, NA)),
            dma((2, 2, NA)),
            dma((2, 2, NB)),
            dma((2, 2, NB)),
            dma((4,)),
            dma((4,)),
        ],
        compiler_params=pltpu.CompilerParams(
            collective_id=identifier, has_side_effects=True, vmem_limit_bytes=40 * 2**20
        ),
        name=f"transport_{cap_a}_{cap_b}",
    )(plan, count, q, cx, cy, area, w, column)


def body(
    tracers,
    courant_x,
    courant_y,
    cell_area,
    neighbor,
    rotation,
    weights,
    sounding_column,
    sounding_count,
):
    vmem, smem = pl.BlockSpec(memory_space=pltpu.VMEM), pl.BlockSpec(memory_space=pltpu.SMEM)
    plan, load = pl.pallas_call(
        plan_kernel,
        out_shape=(
            jax.ShapeDtypeStruct((80, 128), jnp.int32),
            jax.ShapeDtypeStruct((1, 1), jnp.float32),
        ),
        in_specs=[vmem, vmem],
        out_specs=(vmem, smem),
        name="plan",
    )(neighbor.T, rotation.T)
    operands = (
        plan,
        sounding_count,
        tracers[:, 0],
        courant_x[:, 0],
        jnp.swapaxes(courant_y[:, 0], 1, 2),
        cell_area,
        weights,
        sounding_column,
    )
    field, mean = lax.cond(
        load[0, 0] > 0.0,
        functools.partial(run_main, SLOTS, SLOTS, 2),
        functools.partial(run_main, CAP_A, CAP_B, 1),
        *operands,
    )
    return field[:, None], mean


def solution(mesh):
    in_specs = (
        P("tile", "lev", None, None),
        P("tile", "lev", None, None),
        P("tile", "lev", None, None),
        P("tile", None, None),
        P(),
        P(),
        P("tile", "lev", None),
        P("tile", None),
        P("tile"),
    )
    out_specs = (P("tile", "lev", None, None), P("tile", None, None))
    return jax.shard_map(body, mesh=mesh, in_specs=in_specs, out_specs=out_specs, check_vma=False)
```

```python
import functools

import jax
import jax.numpy as jnp
from jax import lax
from jax.experimental import pallas as pl
from jax.experimental.pallas import tpu as pltpu
from jax.sharding import PartitionSpec as P

MESH = pl.DeviceIdType.MESH
STEPS = 2
TILES_DEV = 3
S = 64
TR = 16
W = S * TR
BLOCKS = W // 128
ROWS = S // 8
NA = 16
NB = 8
SLOTS = 12
CAP_A = 2
CAP_B = 4
ROUNDS = 14
INSIDE = (NA + NB) * SLOTS


def lane_gather(x, index):
    return jnp.take_along_axis(x, index, axis=1, mode="promise_in_bounds")


def iota(shape, axis):
    return lax.broadcasted_iota(jnp.int32, shape, axis)


def plan_kernel(nb_ref, rot_ref, plan_ref, load_ref):
    me = lax.axis_index("tile")
    my_a, my_b = lax.rem(me, NA), me // NA
    code = nb_ref[...] * 8 + rot_ref[...]
    flat = jnp.concatenate([code, jnp.zeros(code.shape, jnp.int32)], axis=0)
    sub, lane = iota((8, 128), 0), iota((8, 128), 1)
    edges = []
    for r in range(TILES_DEV):
        at = lane * TILES_DEV + r
        picked = jnp.zeros((8, 128), jnp.int32)
        for block in range(TILES_DEV):
            local = at - 128 * block
            inside = (local >= 0) & (local < 128)
            got = lane_gather(flat[:, 128 * block : 128 * block + 128], jnp.where(inside, local, 0))
            picked = jnp.where(inside, got, picked)
        edges.append(picked[0:4])
    table = jnp.concatenate(edges + [jnp.zeros((4, 128), jnp.int32)], axis=0)
    row = iota((16, 128), 0)
    place = iota((16, 128), 1)
    real = row < SLOTS
    tile = table >> 3
    device = (tile * 21846) >> 16
    slot = (tile - device * TILES_DEV) * 4 + (table & 3)
    flip = (table >> 2) & 1
    dev_a = jnp.where(real, device & (NA - 1), -1)
    dev_b = jnp.where(real, device >> 4, -1)
    use_a = jnp.where(real & (dev_a != (place & (NA - 1))), 1, 0)
    use_b = jnp.where(real & (dev_b != (place >> 4)), 1, 0)
    outside = jnp.maximum(use_a, use_b)

    def partner(x):
        parts = []
        for half in range(2):
            part = slice(8 * half, 8 * half + 8)
            got = jnp.zeros((8, 128), jnp.int32)
            for j in range(SLOTS):
                source = jnp.broadcast_to(x[j : j + 1, :], (8, 128))
                got = jnp.where(slot[part] == j, lane_gather(source, device[part]), got)
            parts.append(got)
        return jnp.concatenate(parts, axis=0)

    def count(key, of):
        every, ahead = jnp.zeros((16, 128), jnp.int32), jnp.zeros((16, 128), jnp.int32)
        for j in range(SLOTS):
            one = slice(j, j + 1)
            same = jnp.where(key == key[one], of[one], 0)
            every += same
            ahead += jnp.where(row > j, same, 0)
        return every, ahead

    own, other = place * SLOTS + row, device * SLOTS + slot
    mix = jnp.minimum(own, other) * 5 + jnp.maximum(own, other) * 3
    by_a = jnp.where(own < other, 1, 0) ^ ((mix >> 2) & 1)
    for turn in range(ROUNDS):
        all_a, ahead_a = count(dev_a, by_a * use_a)
        all_b, ahead_b = count(dev_b, (1 - by_a) * use_b)
        first = by_a == 1
        high_a, high_b = (ahead_a + 1, ahead_b + 1) if turn < 2 else (all_a, all_b)
        late = jnp.where(
            first, jnp.where(high_a > CAP_A, use_a, 0), jnp.where(high_b > CAP_B, use_b, 0)
        )
        over_a, more_a = jnp.maximum(all_a - CAP_A, 0), jnp.maximum(all_a + 1 - CAP_A, 0)
        over_b, more_b = jnp.maximum(all_b - CAP_B, 0), jnp.maximum(all_b + 1 - CAP_B, 0)
        gain = jnp.where(
            first, over_a * use_a - more_b * use_b, over_b * use_b - more_a * use_a
        )
        theirs = partner((gain + 64) * 2 + late)
        wanted = late | (theirs & 1)
        least = 1 if turn < 2 else 0
        better = gain + (theirs >> 1) - 64 >= least
        now = (mix >> 1) + turn if turn < 2 else (mix * 7919 + turn * 104729) >> 5
        by_a = jnp.where(better & (now & 1 == 0), by_a ^ (wanted & outside), by_a)

    go_a, go_b = by_a * outside, (1 - by_a) * outside
    rank_a, rank_b = count(dev_a, go_a)[1], count(dev_b, go_b)[1]
    theirs = partner(rank_a * 16 + rank_b)
    at_a = dev_a * SLOTS + (theirs >> 4)
    at_b = dev_b * SLOTS + (theirs & 15)

    def mine(x):
        index = jnp.full((8, 128), me, jnp.int32)
        return jnp.concatenate([lane_gather(x[0:8], index), lane_gather(x[8:16], index)], axis=0)

    key_a = jnp.where(go_a == 1, dev_a * 16 + rank_a, -1)
    key_b = jnp.where(go_b == 1, dev_b * 16 + rank_b, -1)
    my_key_a, my_key_b = mine(key_a), mine(key_b)
    pack_a, pack_b, forward_a, forward_b = (jnp.zeros((16, 128), jnp.int32) for _ in range(4))
    for j in range(SLOTS):
        one = slice(j, j + 1)
        pack_a += jnp.where(my_key_a[one] == place * 16 + row, j, 0)
        pack_b += jnp.where(my_key_b[one] == place * 16 + row, j, 0)
        forward_a += jnp.where(key_a[one] == my_a * 16 + row, at_b[one], 0)
        forward_b += jnp.where(key_b[one] == my_b * 16 + row, at_a[one], 0)
    take = jnp.where(
        go_a == 1,
        NB * SLOTS + dev_a * SLOTS + rank_a,
        jnp.where(go_b == 1, dev_b * SLOTS + rank_b, (NA + NB) * SLOTS + slot),
    )
    plan_ref[0:16, :] = pack_a
    plan_ref[16:32, :] = pack_b
    plan_ref[32:48, :] = forward_a
    plan_ref[48:64, :] = forward_b
    plan_ref[64:80, :] = mine(jnp.where(real, take * 2 + flip, 0))
    full_a = jnp.where((go_a * use_a == 1) & (rank_a >= CAP_A), 1.0, 0.0)
    full_b = jnp.where((go_b * use_b == 1) & (rank_b >= CAP_B), 1.0, 0.0)
    load_ref[0, 0] = jnp.max(jnp.maximum(full_a, full_b))


def main_kernel(
    cap_a,
    cap_b,
    plan_ref,
    count_ref,
    q_ref,
    cx_ref,
    cy_ref,
    area_ref,
    w_ref,
    column_ref,
    out_ref,
    mean_ref,
    field,
    coef,
    strips,
    send_a,
    send_b,
    got_a0,
    got_a1,
    got_b0,
    got_b1,
    arrived0,
    arrived1,
    level_sum,
    sem_sa,
    sem_ra,
    sem_sb,
    sem_rb,
    sem_sl,
    sem_rl,
):
    me, lev = lax.axis_index("tile"), lax.axis_index("lev")
    my_a, my_b = lax.rem(me, NA), me // NA
    my_z, my_x = my_a // 4, lax.rem(my_a, 4)
    shifts = sorted(range(1, NA), key=lambda k: -2 * min(k // 4, 4 - k // 4) - min(k % 4, 4 - k % 4))
    peers_a = {k: lax.rem(my_z + k // 4, 4) * 4 + lax.rem(my_x + k % 4, 4) for k in shifts}
    peers_b = {k: lax.rem(my_b + k, NB) for k in sorted(range(1, NB), key=lambda k: -min(k, NB - k))}
    peers_l = [lax.rem(lev + k, 4) for k in range(4)]
    got_a, got_b, arrived = (got_a0, got_a1), (got_b0, got_b1), (arrived0, arrived1)

    barrier = pltpu.get_barrier_semaphore()
    everyone = [(my_b * NA + a, lev) for a in peers_a.values()]
    everyone += [(b * NA + my_a, lev) for b in peers_b.values()]
    everyone += [(me, other) for other in peers_l[1:]]
    for target in everyone:
        pl.semaphore_signal(barrier, inc=1, device_id=target, device_id_type=MESH)

    sub, lane = iota((8, 128), 0), iota((8, 128), 1)
    group, member = lane // TR, lane % TR
    last = 128 - TR

    for t in range(TILES_DEV):
        for step in range(STEPS):
            for at in (7, 72):
                field[step, t, at : at + 1, :] = jnp.zeros((1, W), jnp.float32)
        field[0, t, 8:72, :] = q_ref[t]

    def cut_strips(step):
        for t in range(TILES_DEV):
            for r in range(ROWS):
                rows = slice(8 + 8 * r, 16 + 8 * r)
                for e, start, shift in ((0, 0, 0), (1, W - 128, last)):
                    block = field[step, t, rows, start : start + 128]
                    spread = lane_gather(block, member + shift)
                    line = jnp.sum(jnp.where(group == sub, spread, 0.0), axis=0, keepdims=True)
                    strips[4 * t + e, r : r + 1, :] = line
                block = slice(128 * r, 128 * r + 128)
                strips[4 * t + 2, r : r + 1, :] = field[step, t, 8:9, block]
                strips[4 * t + 3, r : r + 1, :] = field[step, t, 71:72, block]

    def send(peers, cap, lane_of, first, source, ref, dst, base, sems, target):
        copies = []
        for k, peer in peers.items():
            for n in range(cap):
                ref[peer, n] = source[plan_ref[first + n, lane_of(peer)]]
            copies.append(
                pltpu.make_async_remote_copy(
                    src_ref=ref.at[peer, pl.ds(0, cap)],
                    dst_ref=dst.at[pl.ds(base, cap)],
                    send_sem=sems[0].at[k],
                    recv_sem=sems[1].at[k],
                    device_id=target(peer),
                    device_id_type=MESH,
                )
            )
            if len(copies) > 1:
                copies[-2].start()
        copies[-1].start()
        return copies

    def send_in_plane(hop, step, first, lane_of, source, dst, base):
        return send(
            peers_a,
            cap_a,
            lane_of,
            first,
            source,
            send_a.at[hop, step],
            dst,
            base + my_a * SLOTS,
            (sem_sa.at[hop, step], sem_ra.at[hop, step]),
            lambda peer: (my_b * NA + peer, lev),
        )

    def send_along_y(hop, step, first, lane_of, source, dst, base):
        return send(
            peers_b,
            cap_b,
            lane_of,
            first,
            source,
            send_b.at[hop, step],
            dst,
            base + my_b * SLOTS,
            (sem_sb.at[hop, step], sem_rb.at[hop, step]),
            lambda peer: (peer * NA + my_a, lev),
        )

    def keep(first, lane, source, to, base):
        for n in range(SLOTS):
            to[base + n] = source[plan_ref[first + n, lane]]

    def exchange(step, meanwhile):
        here = arrived[step]
        one_a = send_in_plane(0, step, 0, lambda a: a, strips, got_a[step], 0)
        one_b = send_along_y(0, step, 16, lambda b: b, strips, got_b[step], 0)
        keep(0, my_a, strips, got_a[step], my_a * SLOTS)
        keep(16, my_b, strips, got_b[step], my_b * SLOTS)
        for k in range(SLOTS):
            here[INSIDE + k] = strips[k]
        meanwhile()
        for copy in one_b:
            copy.wait_recv()
        two_a = send_in_plane(
            1, step, 32, lambda a: my_b * NA + a, got_b[step], here, NB * SLOTS
        )
        keep(32, me, got_b[step], here, NB * SLOTS + my_a * SLOTS)
        for copy in one_a:
            copy.wait_recv()
        two_b = send_along_y(1, step, 48, lambda b: b * NA + my_a, got_a[step], here, 0)
        keep(48, me, got_a[step], here, my_b * SLOTS)
        for copy in two_b + two_a:
            copy.wait_recv()
        return one_a + one_b + two_a + two_b

    def add_halos(step, read, write):
        for t in range(TILES_DEV):
            for e in range(4):
                i = 4 * t + e
                taken = plan_ref[64 + i, 0]
                strip = arrived[step][taken >> 1]
                turned = lane_gather(strip, last - TR * group + member)
                flipped = jnp.full((1, 128), taken & 1, jnp.int32) == 1
                for r in range(ROWS):
                    line = jnp.where(flipped, turned[7 - r : 8 - r], strip[r : r + 1])
                    if e < 2:
                        rows = slice(8 * r, 8 * r + 8)
                        block = slice(0, 128) if e == 0 else slice(W - 128, W)
                        edge = lane < TR if e == 0 else lane >= last
                        spread = lane_gather(jnp.broadcast_to(line, (8, 128)), TR * sub + member)
                        more = jnp.where(edge, spread, 0.0)
                    else:
                        rows = slice(0, 1) if e == 2 else slice(S - 1, S)
                        block = slice(128 * r, 128 * r + 128)
                        more = line
                    write(t, rows, block, read(t, rows, block) + more * coef[1 + e, t, rows, block])

    def coefficients():
        at, to = iota((4 * S, W), 0), iota((4 * S, W), 1)
        repeat = jnp.where(((at & (S - 1)) == (to >> 4)) & (at < 3 * S), 1.0, 0.0)
        repeat = repeat.astype(jnp.bfloat16)
        for t in range(TILES_DEV):
            over = 1.0 / area_ref[t]
            cx, cy = cx_ref[t], cy_ref[t].T
            west, east = cx[:, 0:S], cx[:, 1 : S + 1]
            south, north = cy[0:S], cy[1 : S + 1]
            out = (jnp.maximum(east, 0.0) - jnp.minimum(west, 0.0)) + (
                jnp.maximum(north, 0.0) - jnp.minimum(south, 0.0)
            )
            compact = (
                1.0 - out * over,
                jnp.maximum(west, 0.0) * over,
                -jnp.minimum(east, 0.0) * over,
                jnp.maximum(south, 0.0) * over,
                -jnp.minimum(north, 0.0) * over,
            )
            for n, value in enumerate(compact):
                high = value.astype(jnp.bfloat16).astype(jnp.float32)
                rest = value - high
                middle = rest.astype(jnp.bfloat16).astype(jnp.float32)
                parts = [high, middle, rest - middle, jnp.zeros((S, S), jnp.float32)]
                parts = jnp.concatenate(parts, axis=1).astype(jnp.bfloat16)
                coef[n, t] = jnp.dot(parts, repeat, preferred_element_type=jnp.float32)

    def advance(step, write):
        for t in range(TILES_DEV):
            for r in range(ROWS):
                rows = slice(8 * r, 8 * r + 8)
                top = 8 + 8 * r
                cells = [
                    field[step, t, top : top + 8, 128 * b : 128 * b + 128] for b in range(BLOCKS)
                ]
                up = [pltpu.roll(cell, TR, axis=1) for cell in cells]
                down = [pltpu.roll(cell, 128 - TR, axis=1) for cell in cells]
                for b in range(BLOCKS):
                    block = slice(128 * b, 128 * b + 128)
                    before = up[b - 1] if b > 0 else 0.0
                    after = down[b + 1] if b < BLOCKS - 1 else 0.0
                    west = jnp.where(lane < TR, before, up[b])
                    east = jnp.where(lane >= last, after, down[b])
                    south = field[step, t, top - 1 : top + 7, block]
                    north = field[step, t, top + 1 : top + 9, block]
                    value = (
                        cells[b] * coef[0, t, rows, block]
                        + (west * coef[1, t, rows, block] + east * coef[2, t, rows, block])
                        + (south * coef[3, t, rows, block] + north * coef[4, t, rows, block])
                    )
                    write(t, rows, block, value)

    def read_next(t, rows, block):
        return field[1, t, rows.start + 8 : rows.stop + 8, block]

    def write_next(t, rows, block, value):
        field[1, t, rows.start + 8 : rows.stop + 8, block] = value

    def read_out(t, rows, block):
        return out_ref[t, rows, block]

    def write_out(t, rows, block, value):
        out_ref[t, rows, block] = value

    def first_update():
        coefficients()
        advance(0, write_next)

    def second_update():
        advance(1, write_out)

    cut_strips(0)
    pl.semaphore_wait(barrier, len(everyone))
    sent = []
    for step in range(STEPS):
        if step > 0:
            cut_strips(step)
        sent += exchange(step, first_update if step == 0 else second_update)
        if step == 0:
            add_halos(step, read_next, write_next)
        else:
            add_halos(step, read_out, write_out)

    mine = level_sum.at[lev]
    for t in range(TILES_DEV):
        column = column_ref[t : t + 1, :]
        weight = w_ref[t]
        pick = jnp.where(iota((S, 128), 0) == (column >> 6), 1.0, 0.0)
        at = column & (S - 1)
        total = jnp.zeros((TR, 128), jnp.float32)
        for b in range(BLOCKS):
            turned = out_ref[t, :, 128 * b : 128 * b + 128].T
            rows = jnp.dot(
                turned,
                pick,
                preferred_element_type=jnp.float32,
                precision=lax.Precision.HIGHEST,
            )
            for c in range(8):
                total += jnp.where(at == 8 * b + c, rows[TR * c : TR * c + TR], 0.0)
        mine[t, 0:TR, :] = total * weight
        mine[t, TR : TR + 8, :] = jnp.broadcast_to(weight, (8, 128))
    copies = []
    for k in range(1, 4):
        copies.append(
            pltpu.make_async_remote_copy(
                src_ref=level_sum.at[lev],
                dst_ref=level_sum.at[lev],
                send_sem=sem_sl.at[k],
                recv_sem=sem_rl.at[k],
                device_id=(me, peers_l[k]),
                device_id_type=MESH,
            )
        )
        copies[-1].start()
    sent += copies
    for copy in copies:
        copy.wait_recv()
    for t in range(TILES_DEV):
        total = (level_sum[0, t] + level_sum[1, t]) + (level_sum[2, t] + level_sum[3, t])
        live = iota((TR, 128), 1) < count_ref[t]
        mean_ref[t] = jnp.where(live, total[0:TR] / total[TR : TR + 1], 0.0)
    for copy in sent:
        copy.wait_send()


def run_main(cap_a, cap_b, identifier, plan, count, q, cx, cy, area, w, column):
    vmem, smem = pl.BlockSpec(memory_space=pltpu.VMEM), pl.BlockSpec(memory_space=pltpu.SMEM)
    f32 = jnp.float32
    dma = pltpu.SemaphoreType.DMA
    return pl.pallas_call(
        functools.partial(main_kernel, cap_a, cap_b),
        out_shape=(
            jax.ShapeDtypeStruct((TILES_DEV, S, W), f32),
            jax.ShapeDtypeStruct((TILES_DEV, TR, 128), f32),
        ),
        in_specs=[smem] * 2 + [vmem] * 6,
        out_specs=(vmem, vmem),
        scratch_shapes=[
            pltpu.VMEM((2, TILES_DEV, S + 16, W), f32),
            pltpu.VMEM((5, TILES_DEV, S, W), f32),
            pltpu.VMEM((SLOTS, 8, 128), f32),
            pltpu.VMEM((2, 2, NA, SLOTS, 8, 128), f32),
            pltpu.VMEM((2, 2, NB, SLOTS, 8, 128), f32),
            pltpu.VMEM((NA * SLOTS, 8, 128), f32),
            pltpu.VMEM((NA * SLOTS, 8, 128), f32),
            pltpu.VMEM((NB * SLOTS, 8, 128), f32),
            pltpu.VMEM((NB * SLOTS, 8, 128), f32),
            pltpu.VMEM((INSIDE + SLOTS, 8, 128), f32),
            pltpu.VMEM((INSIDE + SLOTS, 8, 128), f32),
            pltpu.VMEM((4, TILES_DEV, TR + 8, 128), f32),
            dma((2, 2, NA)),
            dma((2, 2, NA)),
            dma((2, 2, NB)),
            dma((2, 2, NB)),
            dma((4,)),
            dma((4,)),
        ],
        compiler_params=pltpu.CompilerParams(
            collective_id=identifier, has_side_effects=True, vmem_limit_bytes=40 * 2**20
        ),
        name=f"transport_{cap_a}_{cap_b}",
    )(plan, count, q, cx, cy, area, w, column)


def body(
    tracers,
    courant_x,
    courant_y,
    cell_area,
    neighbor,
    rotation,
    weights,
    sounding_column,
    sounding_count,
):
    vmem, smem = pl.BlockSpec(memory_space=pltpu.VMEM), pl.BlockSpec(memory_space=pltpu.SMEM)
    plan, load = pl.pallas_call(
        plan_kernel,
        out_shape=(
            jax.ShapeDtypeStruct((80, 128), jnp.int32),
            jax.ShapeDtypeStruct((1, 1), jnp.float32),
        ),
        in_specs=[vmem, vmem],
        out_specs=(vmem, smem),
        name="plan",
    )(neighbor.T, rotation.T)
    operands = (
        plan,
        sounding_count,
        tracers[:, 0],
        courant_x[:, 0],
        jnp.swapaxes(courant_y[:, 0], 1, 2),
        cell_area,
        weights,
        sounding_column,
    )
    field, mean = lax.cond(
        load[0, 0] > 0.0,
        functools.partial(run_main, SLOTS, SLOTS, 2),
        functools.partial(run_main, CAP_A, CAP_B, 1),
        *operands,
    )
    return field[:, None], mean


def solution(mesh):
    in_specs = (
        P("tile", "lev", None, None),
        P("tile", "lev", None, None),
        P("tile", "lev", None, None),
        P("tile", None, None),
        P(),
        P(),
        P("tile", "lev", None),
        P("tile", None),
        P("tile"),
    )
    out_specs = (P("tile", "lev", None, None), P("tile", None, None))
    return jax.shard_map(body, mesh=mesh, in_specs=in_specs, out_specs=out_specs, check_vma=False)
```
